256 devices in a mesh: pr: 32 (over x, z_lo, core), pc: 8 (over y, z_hi).
Axes of the slice: x: 4, y: 4, z: 8 (z_hi: 2, z_lo: 4; z = z_hi * 4 + z_lo), core: 2. Of those that a mesh axis runs over, the one named last changes fastest.
Arguments:
- root_inverse: bfloat16 [6144, 6144], P('pr', 'pc'), may hold values from -6 to 6
- child_panel: bfloat16 [6144, 3072], P('pr', 'pc'), may hold values from -0.078125 to 0.078125
- child_pivots: bfloat16 [3072, 3072], P('pr', 'pc'), may hold values from -6 to 6
- grand_panel_child: bfloat16 [3072, 2048], P('pr', 'pc'), may hold values from -0.0625 to 0.0625
- grand_panel_root: bfloat16 [6144, 2048], P('pr', 'pc'), may hold values from -0.0625 to 0.0625
- grand_pivots: bfloat16 [2048, 2048], P('pr', 'pc'), may hold values from -6 to 6
- root_blocks: int32 [96], replicated, may hold values 0 or 1
Outputs:
- inv_root_child: bfloat16 [6144, 3072], P('pr', 'pc')
- inv_child: bfloat16 [3072, 3072], P('pr', 'pc')
- inv_grand_child: bfloat16 [2048, 3072], P('pr', 'pc')
- inv_root_grand: bfloat16 [6144, 2048], P('pr', 'pc')
- inv_grand: bfloat16 [2048, 2048], P('pr', 'pc')
The draws below stay inside these ranges and needn't reach their ends.
All inputs are finite; a program needn't handle non-finite values.
Results may differ from the reference program's by a relative error of at most 0.0055.
Values may be sent and summed in bfloat16 or wider, within the bound.
A program may use at most 64 MiB of HBM per device.

```python
import jax
import jax.numpy as jnp

NR = 6144
NK = 3072
NJ = 2048
BLK = 64


def set_ends(array, rng, least, largest):
    longest = array.shape.index(max(array.shape))
    spots = []
    for shift in (0, 1):
        where = [jax.random.randint(jax.random.fold_in(rng, axis), (), 0, length) for axis, length in enumerate(array.shape)]
        where[longest] = (where[longest] + shift) % array.shape[longest]
        spots.append(tuple(where))
    return array.at[spots[0]].set(least).at[spots[1]].set(largest)


def block_scale(key, shape, cuts, smallest, top_value):
    def one(dim, blocks):
        steps = jax.random.uniform(jax.random.fold_in(jax.random.fold_in(key, 6), dim), (blocks,), jnp.float32, smallest / len(cuts), top_value / len(cuts))
        return jnp.repeat(jnp.exp(steps), shape[dim] // blocks).reshape((-1,) + (1,) * (len(shape) - dim - 1))

    gain = one(*cuts[0])
    for cut in cuts[1:]:
        gain = gain * one(*cut)
    return gain


def gaussian(key, dims, spread, bound, shards=(), held_as=jnp.bfloat16):
    result = jax.random.normal(key, dims, jnp.float32) * spread
    if len(shards) > 0:
        result = block_scale(key, dims, shards, -0.22, 0.18) * result
    return jnp.clip(result, min=-bound, max=bound).astype(held_as)


def setup_inputs(seed: int = 0) -> dict:
    key_of = jax.random.split(jax.random.key(seed), 8)
    return {
        "root_inverse": gaussian(key_of[0], (NR, NR), 1.0, 6.0, ((0, 32), (1, 8))),
        "child_panel": gaussian(key_of[1], (NR, NK), NR ** -0.5, 0.078125, ((0, 32), (1, 8))),
        "child_pivots": gaussian(key_of[2], (NK, NK), 1.0, 6.0, ((0, 32), (1, 8))),
        "grand_panel_child": gaussian(key_of[3], (NK, NJ), (NK + NR) ** -0.5, 0.0625, ((0, 32), (1, 8))),
        "grand_panel_root": gaussian(key_of[4], (NR, NJ), (NK + NR) ** -0.5, 0.0625, ((0, 32), (1, 8))),
        "grand_pivots": gaussian(key_of[5], (NJ, NJ), 1.0, 6.0, ((0, 32), (1, 8))),
        "root_blocks": set_ends((jax.random.randint(key_of[6], (NR // BLK,), 0, 4) < 3).astype(jnp.int32), jax.random.fold_in(key_of[6], 1), 0, 1),
    }


def reference(root_inverse, child_panel, child_pivots, grand_panel_child, grand_panel_root, grand_pivots, root_blocks):
    kept_rows = (jnp.repeat(root_blocks, BLK) > 0)[:, None]
    near_panel = jnp.where(kept_rows, child_panel, jnp.zeros_like(child_panel))
    far_panel = jnp.where(kept_rows, grand_panel_root, jnp.zeros_like(grand_panel_root))
    product = jnp.dot(root_inverse, near_panel, preferred_element_type=jnp.float32)
    root_child = jnp.where(kept_rows, -product, jnp.zeros_like(product)).astype(jnp.bfloat16)
    child_block = (child_pivots.astype(jnp.float32) - jnp.dot(root_child.T, near_panel, preferred_element_type=jnp.float32)).astype(jnp.bfloat16)
    grand_child = -(jnp.dot(grand_panel_child.T, child_block, preferred_element_type=jnp.float32) + jnp.dot(far_panel.T, root_child, preferred_element_type=jnp.float32))
    grand_child = grand_child.astype(jnp.bfloat16)
    summed = jnp.dot(root_child, grand_panel_child, preferred_element_type=jnp.float32) + jnp.dot(root_inverse, far_panel, preferred_element_type=jnp.float32)
    root_grand = jnp.where(kept_rows, -summed, jnp.zeros_like(summed)).astype(jnp.bfloat16)
    grand_block = grand_pivots.astype(jnp.float32) - jnp.dot(grand_child, grand_panel_child, preferred_element_type=jnp.float32) - jnp.dot(root_grand.T, far_panel, preferred_element_type=jnp.float32)
    return root_child, child_block, grand_child, root_grand, grand_block.astype(jnp.bfloat16)
```

```python
import functools

import jax
import jax.numpy as jnp
from jax import lax
from jax.experimental import pallas as pl
from jax.experimental.pallas import tpu as pltpu
from jax.sharding import PartitionSpec as P

MESH = pl.DeviceIdType.MESH
BF = jnp.bfloat16
F32 = jnp.float32
NSEM = 160


def dot(a, b):
    return jnp.dot(a, b, preferred_element_type=F32)


def tdot(a, b):
    return lax.dot_general(a, b, (((0,), (0,)), ((), ())), preferred_element_type=F32)


def device(x, l, c, y, h):
    return (x * 8 + l * 2 + c, y * 2 + h)


def kernel(
    flags, root, child, cpiv, gchild, groot, gpiv,
    o_rc, o_cc, o_gc, o_rg, o_gg,
    pbuf, rbuf, gcol, gstrip, fstrip, rcs, rgs, gcs, yacc, yg,
    cc_t, cc_ss, cc_sr, cc_xs, cc_xr, cc_a, cc_zs, cc_zr,
    gc_t, gc_ss, gc_sr, gc_xs, gc_xr, gc_a, gc_zs, gc_zr,
    gg_t, gg_ss, gg_sr, gg_xs, gg_xr, gg_a, gg_zs, gg_zr,
    ssem, rsem,
):
    i = lax.axis_index("pr")
    j = lax.axis_index("pc")
    x, l, c = i // 8, (i // 2) % 4, i % 2
    y, h = j // 2, j % 2
    sib = device(x, l, 1 - c, y, h)
    far = device(x, l, c, y, 1 - h)

    def at_x(d):
        return device((x + d) % 4, l, c, y, h)

    def at_y(d):
        return device(x, l, c, (y + d) % 4, h)

    def at_z(d):
        return device(x, (l + d) % 4, c, y, h)

    peers = [sib, far] + [f(d) for f in (at_x, at_y, at_z) for d in (1, 2, 3)]
    barrier = pltpu.get_barrier_semaphore()
    for p in peers:
        pl.semaphore_signal(barrier, inc=1, device_id=p, device_id_type=MESH)

    keep = [jnp.where(flags[i * 3 + q] > 0, 1.0, 0.0).astype(F32) for q in range(3)]
    mine = pbuf.at[x, l, c]
    for q in range(3):
        rows = slice(q * 64, q * 64 + 64)
        mine[rows, 0:384] = (child[rows, :].astype(F32) * keep[q]).astype(BF)
        mine[rows, 384:640] = (groot[rows, :].astype(F32) * keep[q]).astype(BF)
    rbuf[j] = root[...]
    gcol[x, l, c] = gchild[...]
    gstrip[j] = gchild[...]
    fstrip[j] = mine[:, 384:640]
    pl.semaphore_wait(barrier, len(peers))

    started = []

    def send(src, dst, dev):
        n = len(started)
        copy = pltpu.make_async_remote_copy(
            src_ref=src, dst_ref=dst, send_sem=ssem.at[n], recv_sem=rsem.at[n],
            device_id=dev, device_id_type=MESH,
        )
        copy.start()
        started.append(copy)
        return copy

    def same(ref, dev):
        return send(ref, ref, dev)

    def pc_start(buf):
        return [same(buf.at[j], far)], [same(buf.at[j], at_y(d)) for d in (1, 3, 2)]

    def pc_mid(state, buf):
        state[0][0].wait_recv()
        state[1].extend(same(buf.at[y * 2 + 1 - h], at_y(d)) for d in (1, 3, 2))

    def pc_end(state):
        for copy in state[1]:
            copy.wait_recv()

    pz = [same(mine, at_z(d)) for d in (1, 3, 2)]
    r_state = pc_start(rbuf)
    right, left = [same(mine, at_x(1))], [same(mine, at_x(3))]
    for k, d in enumerate((1, 3, 2)):
        pz[k].wait_recv()
        got = pbuf.at[x, (l + 4 - d) % 4, c]
        right.append(same(got, at_x(1)))
        left.append(same(got, at_x(3)))
        if k == 0:
            pc_mid(r_state, rbuf)
    p_own = same(pbuf.at[x, :, c], sib)
    gz = [same(gcol.at[x, l, c], at_z(d)) for d in (1, 3, 2)]
    f_state = pc_start(fstrip)
    g_state = pc_start(gstrip)
    far_r, far_l = [], []
    for k, d in enumerate((0, 1, 3, 2)):
        lz = (l + 4 - d) % 4
        right[k].wait_recv()
        far_r.append(same(pbuf.at[(x + 3) % 4, lz, c, pl.ds(0, 96)], at_x(1)))
        left[k].wait_recv()
        far_l.append(same(pbuf.at[(x + 1) % 4, lz, c, pl.ds(96, 96)], at_x(3)))
    p_left = same(pbuf.at[(x + 3) % 4, :, c], sib)
    p_right = same(pbuf.at[(x + 1) % 4, :, c], sib)
    pc_mid(f_state, fstrip)
    pc_mid(g_state, gstrip)
    for copy in gz:
        copy.wait_recv()
    gx = [same(gcol.at[x, :, c], at_x(d)) for d in (1, 3, 2)]
    pc_end(r_state)

    def group(xs, first):
        def step(hh, carry):
            part = dot(rbuf[xs * 2 + hh], pbuf[xs, pl.ds(hh * 2, 2)].reshape(768, 640))
            yacc[...] = yacc[...] + part
            return carry

        if first:
            yacc[...] = jnp.zeros_like(yacc)
        lax.fori_loop(0, 2, step, 0)

    p_own.wait_recv()
    group(x, True)
    p_left.wait_recv()
    group((x + 3) % 4, False)
    p_right.wait_recv()
    group((x + 1) % 4, False)
    for k in range(4):
        far_r[k].wait_recv()
        far_l[k].wait_recv()
    p_far = same(pbuf.at[(x + 2) % 4, :, c], sib)
    p_far.wait_recv()
    group((x + 2) % 4, False)

    for q in range(3):
        rows = slice(q * 64, q * 64 + 64)
        o_rc[rows, :] = (yacc[rows, 0:384] * (-keep[q])).astype(BF)
    rcs[j] = o_rc[...]
    rc_state = pc_start(rcs)
    for copy in gx:
        copy.wait_recv()
    g_sib = same(gcol.at[:, :, c], sib)
    pc_end(f_state)
    pc_end(g_state)

    def partial(t, dst, pairs, height, width, add):
        def step(hh, carry):
            total = None
            for strip, block in pairs:
                part = tdot(strip[t * 2 + hh], block)
                total = part if total is None else total + part
            total = total.reshape(2, 2, height, width)
            if add:
                total = total + dst[t, pl.ds(hh * 2, 2)]
            dst[t, pl.ds(hh * 2, 2)] = total
            return carry

        lax.fori_loop(0, 2, step, 0)

    def rs_core(dx, tot, ss, sr):
        t = (x + dx) % 4
        ss[t] = tot[t, :, 1 - c].astype(BF)
        return send(ss.at[t], sr.at[t], sib)

    def rs_x(dx, copy, tot, sr, xs, xr):
        t = (x + dx) % 4
        copy.wait_recv()
        xs[dx - 1] = (tot[t, :, c] + sr[t].astype(F32)).astype(BF)
        return send(xs.at[dx - 1], xr.at[dx - 1], at_x(dx))

    def rs_z(copy, xcopies, tot, sr, xr, acc, zs, zr):
        copy.wait_recv()
        total = tot[x, :, c] + sr[x].astype(F32)
        for xc in xcopies:
            xc.wait_recv()
        for k in range(3):
            total = total + xr[k].astype(F32)
        acc[...] = total
        zs[...] = total.astype(BF)
        return [send(zs.at[(l + d) % 4], zr.at[d - 1], at_z(d)) for d in (1, 3, 2)]

    def rs_end(copies, acc, zr):
        for copy in copies:
            copy.wait_recv()
        total = acc[l]
        for k in range(3):
            total = total + zr[k].astype(F32)
        return total

    order = (2, 1, 3, 0)

    for t in range(4):
        partial(t, gc_t, [(fstrip, o_rc[...])], 64, 384, False)
    pc_mid(rc_state, rcs)
    g_sib.wait_recv()
    pc_end(rc_state)

    near = mine[:, 0:384]
    cores = []
    for dx in order:
        partial((x + dx) % 4, cc_t, [(rcs, near)], 96, 384, False)
        cores.append(rs_core(dx, cc_t, cc_ss, cc_sr))
    ccx = [rs_x(dx, cores[k], cc_t, cc_sr, cc_xs, cc_xr) for k, dx in enumerate(order[:3])]

    yg[...] = yacc[:, 384:640]

    def rg_step(n, carry):
        panel = gcol[n // 2, pl.ds((n % 2) * 2, 2)].reshape(384, 256)
        yg[...] = yg[...] + dot(rcs[n], panel)
        return carry

    lax.fori_loop(0, 8, rg_step, 0)
    for q in range(3):
        rows = slice(q * 64, q * 64 + 64)
        o_rg[rows, :] = (yg[rows, :] * (-keep[q])).astype(BF)
    rgs[j] = o_rg[...]
    rg_state = pc_start(rgs)

    ccz = rs_z(cores[3], ccx, cc_t, cc_sr, cc_xr, cc_a, cc_zs, cc_zr)
    pc_mid(rg_state, rgs)
    child_sum = rs_end(ccz, cc_a, cc_zr)
    o_cc[...] = (cpiv[...].astype(F32) - child_sum).astype(BF)

    cores = []
    for dx in order:
        partial((x + dx) % 4, gc_t, [(gstrip, o_cc[...])], 64, 384, True)
        cores.append(rs_core(dx, gc_t, gc_ss, gc_sr))
    gcx = [rs_x(dx, cores[k], gc_t, gc_sr, gc_xs, gc_xr) for k, dx in enumerate(order[:3])]

    pc_end(rg_state)
    far_block = mine[:, 384:640]
    gg_cores = []
    for dx in order:
        partial((x + dx) % 4, gg_t, [(rgs, far_block)], 64, 256, False)
        gg_cores.append(rs_core(dx, gg_t, gg_ss, gg_sr))
    ggx = [rs_x(dx, gg_cores[k], gg_t, gg_sr, gg_xs, gg_xr) for k, dx in enumerate(order[:3])]

    gcz = rs_z(cores[3], gcx, gc_t, gc_sr, gc_xr, gc_a, gc_zs, gc_zr)
    ggz = rs_z(gg_cores[3], ggx, gg_t, gg_sr, gg_xr, gg_a, gg_zs, gg_zr)
    cross = rs_end(gcz, gc_a, gc_zr)
    o_gc[...] = (-cross).astype(BF)
    gcs[j] = o_gc[...]
    gc_state = pc_start(gcs)
    farther = rs_end(ggz, gg_a, gg_zr)
    gg_a[0] = gpiv[...].astype(F32) - farther
    pc_mid(gc_state, gcs)
    pc_end(gc_state)

    def gg_step(n, carry):
        panel = gcol[n // 2, pl.ds((n % 2) * 2, 2)].reshape(384, 256)
        gg_a[0] = gg_a[0] - dot(gcs[n], panel)
        return carry

    lax.fori_loop(0, 8, gg_step, 0)
    o_gg[...] = gg_a[0].astype(BF)
    for copy in started:
        copy.wait_send()


def rs_scratch(height, width):
    return [
        pltpu.VMEM((4, 4, 2, height, width), F32),
        pltpu.VMEM((4, 4, height, width), BF),
        pltpu.VMEM((4, 4, height, width), BF),
        pltpu.VMEM((3, 4, height, width), BF),
        pltpu.VMEM((3, 4, height, width), BF),
        pltpu.VMEM((4, height, width), F32),
        pltpu.VMEM((4, height, width), BF),
        pltpu.VMEM((3, height, width), BF),
    ]


def per_device(root, child, cpiv, gchild, groot, gpiv, blocks):
    vm = pl.BlockSpec(memory_space=pltpu.VMEM)
    shapes = [(192, 384), (96, 384), (64, 384), (192, 256), (64, 256)]
    return pl.pallas_call(
        kernel,
        out_shape=[jax.ShapeDtypeStruct(s, BF) for s in shapes],
        in_specs=[pl.BlockSpec(memory_space=pltpu.SMEM)] + [vm] * 6,
        out_specs=[vm] * 5,
        scratch_shapes=[
            pltpu.VMEM((4, 4, 2, 192, 640), BF),
            pltpu.VMEM((8, 192, 768), BF),
            pltpu.VMEM((4, 4, 2, 96, 256), BF),
            pltpu.VMEM((8, 96, 256), BF),
            pltpu.VMEM((8, 192, 256), BF),
            pltpu.VMEM((8, 192, 384), BF),
            pltpu.VMEM((8, 192, 256), BF),
            pltpu.VMEM((8, 64, 384), BF),
            pltpu.VMEM((192, 640), F32),
            pltpu.VMEM((192, 256), F32),
            *rs_scratch(96, 384),
            *rs_scratch(64, 384),
            *rs_scratch(64, 256),
            pltpu.SemaphoreType.DMA((NSEM,)),
            pltpu.SemaphoreType.DMA((NSEM,)),
        ],
        compiler_params=pltpu.CompilerParams(
            collective_id=0, has_side_effects=True, vmem_limit_bytes=50 * 2**20
        ),
        name="selected_inverse",
    )(blocks, root, child, cpiv, gchild, groot, gpiv)


def solution(mesh):
    placed = (P("pr", "pc"),) * 6 + (P(),)
    return jax.shard_map(
        per_device,
        mesh=mesh,
        in_specs=placed,
        out_specs=(P("pr", "pc"),) * 5,
        check_vma=False,
    )
```

```python
import functools

import jax
import jax.numpy as jnp
from jax import lax
from jax.experimental import pallas as pl
from jax.experimental.pallas import tpu as pltpu
from jax.sharding import PartitionSpec as P

MESH = pl.DeviceIdType.MESH
BF = jnp.bfloat16
F32 = jnp.float32
NSEM = 160


def dot(a, b):
    return jnp.dot(a, b, preferred_element_type=F32)


def tdot(a, b):
    return lax.dot_general(a, b, (((0,), (0,)), ((), ())), preferred_element_type=F32)


def device(x, l, c, y, h):
    return (x * 8 + l * 2 + c, y * 2 + h)


def kernel(
    flags, root, child, cpiv, gchild, groot, gpiv,
    o_rc, o_cc, o_gc, o_rg, o_gg,
    craw, fraw, pc_in, pg_in, cb, fb, rbuf, gcol, gstrip, fstrip, rcs, ws, rgs, gcs, yc, yf,
    cc_t, cc_ss, cc_sr, cc_xs, cc_xr, cc_a, cc_zs, cc_zr,
    gc_t, gc_ss, gc_sr, gc_xs, gc_xr, gc_a, gc_zs, gc_zr,
    gg_t, gg_ss, gg_sr, gg_xs, gg_xr, gg_a, gg_zs, gg_zr,
    ssem, rsem, lsem,
):
    i = lax.axis_index("pr")
    j = lax.axis_index("pc")
    x, l, c = i // 8, (i // 2) % 4, i % 2
    y, h = j // 2, j % 2
    sib = device(x, l, 1 - c, y, h)
    far = device(x, l, c, y, 1 - h)

    def at_x(d):
        return device((x + d) % 4, l, c, y, h)

    def at_y(d):
        return device(x, l, c, (y + d) % 4, h)

    def at_z(d):
        return device(x, (l + d) % 4, c, y, h)

    peers = [sib, far] + [f(d) for f in (at_x, at_y, at_z) for d in (1, 2, 3)]
    barrier = pltpu.get_barrier_semaphore()
    for p in peers:
        pl.semaphore_signal(barrier, inc=1, device_id=p, device_id_type=MESH)

    pulls = []
    for src, dst in (
        (child, craw), (root, rbuf.at[j]), (groot, fraw), (gchild, gcol.at[x, l, c]),
        (gchild, gstrip.at[j]), (cpiv, pc_in), (gpiv, pg_in),
    ):
        pull = pltpu.make_async_copy(src, dst, lsem.at[len(pulls)])
        pull.start()
        pulls.append(pull)
    keep = [jnp.where(flags[i * 3 + q] > 0, 1.0, 0.0).astype(F32) for q in range(3)]
    thirds = [slice(q * 64, q * 64 + 64) for q in range(3)]
    c_mine, f_mine = cb.at[x, l, c], fb.at[x, l, c]
    pulls[0].wait()
    for q, rows in enumerate(thirds):
        c_mine[rows, :] = (craw[rows, :].astype(F32) * keep[q]).astype(BF)
    pulls[1].wait()
    pl.semaphore_wait(barrier, len(peers))

    started = []

    def send(src, dst, dev):
        n = len(started)
        copy = pltpu.make_async_remote_copy(
            src_ref=src, dst_ref=dst, send_sem=ssem.at[n], recv_sem=rsem.at[n],
            device_id=dev, device_id_type=MESH,
        )
        copy.start()
        started.append(copy)
        return copy

    def same(ref, dev):
        return send(ref, ref, dev)

    def pc_start(buf):
        return [same(buf.at[j], far)], [same(buf.at[j], at_y(d)) for d in (1, 3, 2)]

    def pc_mid(state, buf):
        state[0][0].wait_recv()
        state[1].extend(same(buf.at[y * 2 + 1 - h], at_y(d)) for d in (1, 3, 2))

    def pc_end(state):
        for copy in state[1]:
            copy.wait_recv()

    upper, lower = pl.ds(0, 96), pl.ds(96, 96)
    y_left, y_right = (y + 3) % 4, (y + 1) % 4

    def r_ring(hh):
        n = y * 2 + hh
        return [
            same(rbuf.at[n, upper], at_y(1)), same(rbuf.at[n, lower], at_y(3)),
            same(rbuf.at[n, upper], at_y(3)), same(rbuf.at[n, lower], at_y(1)),
        ]

    def r_pass(copies, hh):
        copies[0].wait_recv()
        copies.append(same(rbuf.at[y_left * 2 + hh, upper], at_y(1)))
        copies[1].wait_recv()
        copies.append(same(rbuf.at[y_right * 2 + hh, lower], at_y(3)))

    def r_end(copies):
        for copy in copies[2:]:
            copy.wait_recv()

    def z_start(mine):
        return [same(mine, at_z(d)) for d in (1, 3, 2)], [same(mine, at_x(1))], [same(mine, at_x(3))]

    def z_pass(state, buf, k):
        state[0][k].wait_recv()
        got = buf.at[x, (l + 4 - (1, 3, 2)[k]) % 4, c]
        state[1].append(same(got, at_x(1)))
        state[2].append(same(got, at_x(3)))

    def x_pass(state, buf, k, into):
        lz = (l + 4 - (0, 1, 3, 2)[k]) % 4
        state[1][k].wait_recv()
        into.append(same(buf.at[(x + 3) % 4, lz, c, upper], at_x(1)))
        state[2][k].wait_recv()
        into.append(same(buf.at[(x + 1) % 4, lz, c, lower], at_x(3)))

    def to_sib(buf, d):
        return same(buf.at[(x + d) % 4, :, c], sib)

    c_state, c_far = z_start(c_mine), []
    r_own = r_ring(h)
    pulls[2].wait()
    for q, rows in enumerate(thirds):
        f_mine[rows, :] = (fraw[rows, :].astype(F32) * keep[q]).astype(BF)
    fstrip[j] = f_mine[...]
    for k in (3, 4, 5, 6):
        pulls[k].wait()
    z_pass(c_state, cb, 0)
    r_far_a = same(rbuf.at[j, upper], far)
    r_pass(r_own, h)
    z_pass(c_state, cb, 1)
    r_far_b = same(rbuf.at[j, lower], far)
    z_pass(c_state, cb, 2)
    f_state, f_far = z_start(f_mine), []
    gz = [same(gcol.at[x, l, c], at_z(d)) for d in (1, 3, 2)]
    c_sibs = [to_sib(cb, 0)]
    x_pass(c_state, cb, 0, c_far)
    x_pass(c_state, cb, 1, c_far)
    r_far_a.wait_recv()
    n_far = y * 2 + 1 - h
    r_away = [same(rbuf.at[n_far, upper], at_y(1)), same(rbuf.at[n_far, upper], at_y(3))]
    x_pass(c_state, cb, 2, c_far)
    r_far_b.wait_recv()
    r_away += [same(rbuf.at[n_far, lower], at_y(3)), same(rbuf.at[n_far, lower], at_y(1))]
    r_away = [r_away[0], r_away[2], r_away[1], r_away[3]]
    x_pass(c_state, cb, 3, c_far)
    c_sibs += [to_sib(cb, 3), to_sib(cb, 1)]
    fs_state = pc_start(fstrip)
    gs_state = pc_start(gstrip)
    r_pass(r_away, 1 - h)
    for k in range(3):
        z_pass(f_state, fb, k)
    for copy in gz:
        copy.wait_recv()
    gx = [same(gcol.at[x, :, c], at_x(d)) for d in (1, 3, 2)]
    for copy in c_far:
        copy.wait_recv()
    c_sibs.append(to_sib(cb, 2))
    f_sibs = [to_sib(fb, 0)]
    r_end(r_own)
    r_end(r_away)

    def group(buf, acc, xs, width, first):
        def half(hh):
            return dot(rbuf[xs * 2 + hh], buf[xs, pl.ds(hh * 2, 2)].reshape(768, width))

        part = half(0) + half(1)
        acc[...] = part if first else acc[...] + part

    for k, d in enumerate((0, 3, 1, 2)):
        c_sibs[k].wait_recv()
        group(cb, yc, (x + d) % 4, 384, k == 0)

    for q, rows in enumerate(thirds):
        o_rc[rows, :] = (yc[rows, :] * (-keep[q])).astype(BF)
    rcs[j] = o_rc[...]
    rc_state = pc_start(rcs)

    for k in range(4):
        x_pass(f_state, fb, k, f_far)
    f_sibs += [to_sib(fb, 3), to_sib(fb, 1)]
    pc_mid(fs_state, fstrip)
    pc_mid(gs_state, gstrip)
    for copy in gx:
        copy.wait_recv()
    g_sib = same(gcol.at[:, :, c], sib)
    pc_mid(rc_state, rcs)

    def partial(t, dst, pairs, height, add):
        def step(hh, carry):
            total = None
            for strip, block in pairs:
                part = tdot(strip[t * 2 + hh], block)
                total = part if total is None else total + part
            total = total.reshape(2, 2, height, total.shape[-1])
            if add:
                total = dst[t, pl.ds(hh * 2, 2)] - total
            dst[t, pl.ds(hh * 2, 2)] = total
            return carry

        lax.fori_loop(0, 2, step, 0)

    def rs_core(dx, tot, ss, sr):
        t = (x + dx) % 4
        ss[t] = tot[t, :, 1 - c].astype(BF)
        return send(ss.at[t], sr.at[t], sib)

    def rs_x(dx, copy, tot, sr, xs, xr):
        t = (x + dx) % 4
        copy.wait_recv()
        xs[dx - 1] = (tot[t, :, c] + sr[t].astype(F32)).astype(BF)
        return send(xs.at[dx - 1], xr.at[dx - 1], at_x(dx))

    def rs_z(copy, xcopies, tot, sr, xr, acc, zs, zr):
        copy.wait_recv()
        total = tot[x, :, c] + sr[x].astype(F32)
        for xc in xcopies:
            xc.wait_recv()
        for k in range(3):
            total = total + xr[k].astype(F32)
        acc[...] = total
        zs[...] = total.astype(BF)
        return [send(zs.at[(l + d) % 4], zr.at[d - 1], at_z(d)) for d in (1, 3, 2)]

    def rs_end(copies, acc, zr):
        for copy in copies:
            copy.wait_recv()
        total = acc[l]
        for k in range(3):
            total = total + zr[k].astype(F32)
        return total

    order = (2, 1, 3, 0)

    for copy in f_far:
        copy.wait_recv()
    f_sibs.append(to_sib(fb, 2))
    for k, d in enumerate((0, 3, 1, 2)):
        f_sibs[k].wait_recv()
        group(fb, yf, (x + d) % 4, 256, k == 0)
    pc_end(fs_state)
    pc_end(gs_state)
    for t in range(4):
        partial(t, gc_t, [(fstrip, o_rc[...]), (gstrip, pc_in[...])], 64, False)
    g_sib.wait_recv()
    pc_end(rc_state)

    def w_term(n):
        return dot(rcs[n], gcol[n // 2, pl.ds((n % 2) * 2, 2)].reshape(384, 256))

    w = w_term(0)
    for n in range(1, 8):
        w = w + w_term(n)
    ws[j] = w.astype(BF)
    w_state = pc_start(ws)
    yf[...] = yf[...] + w
    for q, rows in enumerate(thirds):
        o_rg[rows, :] = (yf[rows, :] * (-keep[q])).astype(BF)
    rgs[j] = o_rg[...]

    cc_core = []
    for dx in order:
        partial((x + dx) % 4, cc_t, [(rcs, c_mine[...])], 96, False)
        cc_core.append(rs_core(dx, cc_t, cc_ss, cc_sr))
    cc_x = [rs_x(dx, cc_core[k], cc_t, cc_sr, cc_xs, cc_xr) for k, dx in enumerate(order[:3])]

    pc_mid(w_state, ws)
    rg_state = pc_start(rgs)
    pc_mid(rg_state, rgs)

    pc_end(w_state)
    gc_core = []
    for dx in order:
        partial((x + dx) % 4, gc_t, [(ws, c_mine[...])], 64, True)
        gc_core.append(rs_core(dx, gc_t, gc_ss, gc_sr))
    gc_x = [rs_x(dx, gc_core[k], gc_t, gc_sr, gc_xs, gc_xr) for k, dx in enumerate(order[:3])]

    pc_end(rg_state)
    gg_core = []
    for dx in order:
        partial((x + dx) % 4, gg_t, [(rgs, f_mine[...])], 64, False)
        gg_core.append(rs_core(dx, gg_t, gg_ss, gg_sr))
    gg_x = [rs_x(dx, gg_core[k], gg_t, gg_sr, gg_xs, gg_xr) for k, dx in enumerate(order[:3])]

    cc_z = rs_z(cc_core[3], cc_x, cc_t, cc_sr, cc_xr, cc_a, cc_zs, cc_zr)
    gc_z = rs_z(gc_core[3], gc_x, gc_t, gc_sr, gc_xr, gc_a, gc_zs, gc_zr)
    gg_z = rs_z(gg_core[3], gg_x, gg_t, gg_sr, gg_xr, gg_a, gg_zs, gg_zr)
    o_gc[...] = (-rs_end(gc_z, gc_a, gc_zr)).astype(BF)
    gcs[j] = o_gc[...]
    gc_state = pc_start(gcs)
    o_cc[...] = (pc_in[...].astype(F32) - rs_end(cc_z, cc_a, cc_zr)).astype(BF)
    total = pg_in[...].astype(F32) - rs_end(gg_z, gg_a, gg_zr)
    pc_mid(gc_state, gcs)
    pc_end(gc_state)

    for n in range(8):
        panel = gcol[n // 2, pl.ds((n % 2) * 2, 2)].reshape(384, 256)
        total = total - dot(gcs[n], panel)
    o_gg[...] = total.astype(BF)
    for copy in started:
        copy.wait_send()


def rs_scratch(height, width):
    return [
        pltpu.VMEM((4, 4, 2, height, width), F32),
        pltpu.VMEM((4, 4, height, width), BF),
        pltpu.VMEM((4, 4, height, width), BF),
        pltpu.VMEM((3, 4, height, width), BF),
        pltpu.VMEM((3, 4, height, width), BF),
        pltpu.VMEM((4, height, width), F32),
        pltpu.VMEM((4, height, width), BF),
        pltpu.VMEM((3, height, width), BF),
    ]


def per_device(root, child, cpiv, gchild, groot, gpiv, blocks):
    vm = pl.BlockSpec(memory_space=pltpu.VMEM)
    shapes = [(192, 384), (96, 384), (64, 384), (192, 256), (64, 256)]
    return pl.pallas_call(
        kernel,
        out_shape=[jax.ShapeDtypeStruct(s, BF) for s in shapes],
        in_specs=[pl.BlockSpec(memory_space=pltpu.SMEM)] + [pl.BlockSpec(memory_space=pl.ANY)] * 6,
        out_specs=[vm] * 5,
        scratch_shapes=[
            pltpu.VMEM((192, 384), BF),
            pltpu.VMEM((192, 256), BF),
            pltpu.VMEM((96, 384), BF),
            pltpu.VMEM((64, 256), BF),
            pltpu.VMEM((4, 4, 2, 192, 384), BF),
            pltpu.VMEM((4, 4, 2, 192, 256), BF),
            pltpu.VMEM((8, 192, 768), BF),
            pltpu.VMEM((4, 4, 2, 96, 256), BF),
            pltpu.VMEM((8, 96, 256), BF),
            pltpu.VMEM((8, 192, 256), BF),
            pltpu.VMEM((8, 192, 384), BF),
            pltpu.VMEM((8, 192, 256), BF),
            pltpu.VMEM((8, 192, 256), BF),
            pltpu.VMEM((8, 64, 384), BF),
            pltpu.VMEM((192, 384), F32),
            pltpu.VMEM((192, 256), F32),
            *rs_scratch(96, 384),
            *rs_scratch(64, 384),
            *rs_scratch(64, 256),
            pltpu.SemaphoreType.DMA((NSEM,)),
            pltpu.SemaphoreType.DMA((NSEM,)),
            pltpu.SemaphoreType.DMA((7,)),
        ],
        compiler_params=pltpu.CompilerParams(
            collective_id=0, has_side_effects=True, vmem_limit_bytes=62 * 2**20
        ),
        name="selected_inverse",
    )(blocks, root, child, cpiv, gchild, groot, gpiv)


def solution(mesh):
    placed = (P("pr", "pc"),) * 6 + (P(),)
    return jax.shard_map(
        per_device,
        mesh=mesh,
        in_specs=placed,
        out_specs=(P("pr", "pc"),) * 5,
        check_vma=False,
    )
```

```python
import functools

import jax
import jax.numpy as jnp
from jax import lax
from jax.experimental import pallas as pl
from jax.experimental.pallas import tpu as pltpu
from jax.sharding import PartitionSpec as P

MESH = pl.DeviceIdType.MESH
BF = jnp.bfloat16
F32 = jnp.float32
NSEM = 160


def dot(a, b):
    return jnp.dot(a, b, preferred_element_type=F32)


def tdot(a, b):
    return lax.dot_general(a, b, (((0,), (0,)), ((), ())), preferred_element_type=F32)


def device(x, l, c, y, h):
    return (x * 8 + l * 2 + c, y * 2 + h)


def kernel(
    flags, root, child, cpiv, gchild, groot, gpiv,
    o_rc, o_cc, o_gc, o_rg, o_gg,
    craw, fraw, px, cx, fx, pg_in, cb, fb, rbuf, gcol, gstrip, fstrip, rcs, ws, rgs, gcs, yc, yf,
    cc_t, cc_ss, cc_sr, cc_xs, cc_xr, cc_zs, cc_zr,
    gc_t, gc_ss, gc_sr, gc_xs, gc_xr, gc_zs, gc_zr,
    gg_t, gg_ss, gg_sr, gg_xs, gg_xr, gg_zs, gg_zr,
    ssem, rsem, lsem, zssem, zrsem,
):
    i = lax.axis_index("pr")
    j = lax.axis_index("pc")
    x, l, c = i // 8, (i // 2) % 4, i % 2
    y, h = j // 2, j % 2
    sib = device(x, l, 1 - c, y, h)
    far = device(x, l, c, y, 1 - h)

    def at_x(d):
        return device((x + d) % 4, l, c, y, h)

    def at_y(d):
        return device(x, l, c, (y + d) % 4, h)

    def at_z(d):
        return device(x, (l + d) % 4, c, y, h)

    peers = [sib, far] + [f(d) for f in (at_x, at_y, at_z) for d in (1, 2, 3)]
    peers += [device(x, (l + d) % 4, c, y, 1 - h) for d in (1, 2, 3)]
    barrier = pltpu.get_barrier_semaphore()
    for p in peers:
        pl.semaphore_signal(barrier, inc=1, device_id=p, device_id_type=MESH)

    pulls = []
    for src, dst in (
        (child, craw), (root, rbuf.at[j]), (groot, fraw), (gchild, gcol.at[x, l, c]),
        (gchild, gstrip.at[j]), (cpiv, px.at[h]), (gpiv, pg_in),
    ):
        pull = pltpu.make_async_copy(src, dst, lsem.at[len(pulls)])
        pull.start()
        pulls.append(pull)
    keep = [jnp.where(flags[i * 3 + q] > 0, 1.0, 0.0).astype(F32) for q in range(3)]
    thirds = [slice(q * 64, q * 64 + 64) for q in range(3)]
    c_mine, f_mine = cb.at[x, l, c], fb.at[x, l, c]
    pulls[0].wait()
    for q, rows in enumerate(thirds):
        c_mine[rows, :] = (craw[rows, :].astype(F32) * keep[q]).astype(BF)
    cx[h] = c_mine[...]
    pulls[1].wait()
    pl.semaphore_wait(barrier, len(peers))

    started = []

    def send(src, dst, dev):
        n = len(started)
        copy = pltpu.make_async_remote_copy(
            src_ref=src, dst_ref=dst, send_sem=ssem.at[n], recv_sem=rsem.at[n],
            device_id=dev, device_id_type=MESH,
        )
        copy.start()
        started.append(copy)
        return copy

    def same(ref, dev):
        return send(ref, ref, dev)

    def pc_y(buf):
        return [], [same(buf.at[j], at_y(d)) for d in (1, 3, 2)]

    def pc_far(state, buf):
        state[0].append(same(buf.at[j], far))

    def pc_start(buf):
        return [same(buf.at[j], far)], [same(buf.at[j], at_y(d)) for d in (1, 3, 2)]

    def pc_mid(state, buf):
        state[0][0].wait_recv()
        state[1].extend(same(buf.at[y * 2 + 1 - h], at_y(d)) for d in (1, 3, 2))

    def pc_end(state):
        for copy in state[1]:
            copy.wait_recv()

    upper, lower = pl.ds(0, 96), pl.ds(96, 96)
    y_left, y_right = (y + 3) % 4, (y + 1) % 4

    def r_ring(hh):
        n = y * 2 + hh
        return [
            same(rbuf.at[n, upper], at_y(1)), same(rbuf.at[n, lower], at_y(3)),
            same(rbuf.at[n, upper], at_y(3)), same(rbuf.at[n, lower], at_y(1)),
        ]

    def r_pass(copies, hh):
        copies[0].wait_recv()
        copies.append(same(rbuf.at[y_left * 2 + hh, upper], at_y(1)))
        copies[1].wait_recv()
        copies.append(same(rbuf.at[y_right * 2 + hh, lower], at_y(3)))

    def r_end(copies):
        for copy in copies[2:]:
            copy.wait_recv()

    def x_start(mine):
        return [], [same(mine, at_x(1))], [same(mine, at_x(3))]

    def z_start(state, mine):
        state[0].extend(same(mine, at_z(d)) for d in (1, 3, 2))

    def z_pass(state, buf, k):
        state[0][k].wait_recv()
        got = buf.at[x, (l + 4 - (1, 3, 2)[k]) % 4, c]
        state[1].append(same(got, at_x(1)))
        state[2].append(same(got, at_x(3)))

    def x_pass(state, buf, k, into):
        lz = (l + 4 - (0, 1, 3, 2)[k]) % 4
        state[1][k].wait_recv()
        into.append(same(buf.at[(x + 3) % 4, lz, c, upper], at_x(1)))
        state[2][k].wait_recv()
        into.append(same(buf.at[(x + 1) % 4, lz, c, lower], at_x(3)))

    def to_sib(buf, d):
        return same(buf.at[(x + d) % 4, :, c], sib)

    c_state, c_far = x_start(c_mine), []
    z_start(c_state, c_mine)
    r_own = r_ring(h)
    pulls[2].wait()
    for q, rows in enumerate(thirds):
        f_mine[rows, :] = (fraw[rows, :].astype(F32) * keep[q]).astype(BF)
    fstrip[j] = f_mine[...]
    fx[h] = f_mine[...]
    for k in (3, 4, 5, 6):
        pulls[k].wait()
    z_pass(c_state, cb, 0)
    r_far_a = same(rbuf.at[j, upper], far)
    r_pass(r_own, h)
    z_pass(c_state, cb, 1)
    r_far_b = same(rbuf.at[j, lower], far)
    z_pass(c_state, cb, 2)
    c_sibs = [to_sib(cb, 0)]
    x_pass(c_state, cb, 0, c_far)
    x_pass(c_state, cb, 1, c_far)
    r_far_a.wait_recv()
    n_far = y * 2 + 1 - h
    r_away = [same(rbuf.at[n_far, upper], at_y(1)), same(rbuf.at[n_far, upper], at_y(3))]
    x_pass(c_state, cb, 2, c_far)
    r_far_b.wait_recv()
    r_away += [same(rbuf.at[n_far, lower], at_y(3)), same(rbuf.at[n_far, lower], at_y(1))]
    r_away = [r_away[0], r_away[2], r_away[1], r_away[3]]
    x_pass(c_state, cb, 3, c_far)
    c_sibs += [to_sib(cb, 3), to_sib(cb, 1)]
    gz = [same(gcol.at[x, l, c], at_z(d)) for d in (1, 3, 2)]
    r_pass(r_away, 1 - h)
    f_state, f_far = x_start(f_mine), []
    z_start(f_state, f_mine)
    fs_state, gs_state = pc_y(fstrip), pc_y(gstrip)
    for copy in gz:
        copy.wait_recv()
    gx = [same(gcol.at[x, :, c], at_x(d)) for d in (1, 3, 2)]
    for copy in c_far:
        copy.wait_recv()
    c_sibs.append(to_sib(cb, 2))
    z_pass(f_state, fb, 0)
    z_pass(f_state, fb, 1)
    r_end(r_own)
    r_end(r_away)

    def group(buf, acc, xs, width, first):
        def half(hh):
            return dot(rbuf[xs * 2 + hh], buf[xs, pl.ds(hh * 2, 2)].reshape(768, width))

        part = half(0) + half(1)
        acc[...] = part if first else acc[...] + part

    for k, d in enumerate((0, 3, 1, 2)):
        c_sibs[k].wait_recv()
        group(cb, yc, (x + d) % 4, 384, k == 0)

    for q, rows in enumerate(thirds):
        o_rc[rows, :] = (yc[rows, :] * (-keep[q])).astype(BF)
    rcs[j] = o_rc[...]
    rc_state = pc_start(rcs)

    c_swap = same(cx.at[h], far)
    p_swap = same(px.at[h], far)
    f_swap = same(fx.at[h], far)
    z_pass(f_state, fb, 2)
    f_sibs = [to_sib(fb, 0)]

    def partial(t, dst, pairs, height, add):
        strips = [(strip[t * 2 + h].T, block) for strip, block in pairs]
        for v in range(2):
            total = None
            for strip, block in strips:
                part = dot(strip, block(v))
                total = part if total is None else total + part
            total = total.reshape(2, 2, height, total.shape[-1])
            if add:
                total = dst[t, 2 * v : 2 * v + 2] - total
            dst[t, 2 * v : 2 * v + 2] = total

    def rs_core(dx, tot, ss, sr):
        t = (x + dx) % 4
        ss[t] = tot[t, :, 1 - c].astype(BF)
        return send(ss.at[t], sr.at[t], sib)

    def rs_x(dx, copy, tot, sr, xs, xr):
        t = (x + dx) % 4
        copy.wait_recv()
        xs[dx - 1] = (tot[t, :, c] + sr[t].astype(F32)).astype(BF)
        return send(xs.at[dx - 1], xr.at[dx - 1], at_x(dx))

    here = l // 2 == h

    def rs_z(n, copy, xcopies, tot, sr, xr, zs, zr):
        copy.wait_recv()
        total = tot[x, :, c] + sr[x].astype(F32)
        for xc in xcopies:
            xc.wait_recv()
        for k in range(3):
            total = total + xr[k].astype(F32)
        zs[...] = total.astype(BF)
        copies = []
        for m in (3, 2, 1, 0):
            own = jnp.logical_and(here, h * 2 + l % 2 == m)
            copy = pltpu.make_async_remote_copy(
                src_ref=zs.at[m], dst_ref=zr.at[l], send_sem=zssem.at[n, m], recv_sem=zrsem.at[n, l],
                device_id=device(x, 2 * h + m % 2, c, y, m // 2), device_id_type=MESH,
            )

            @pl.when(jnp.logical_not(own))
            def _():
                copy.start()

            @pl.when(own)
            def _():
                zr[l] = zs[m]

            copies.append((copy, own))
        return n, copies

    def rs_end(state, zs, zr):
        n, copies = state
        for k in range(4):
            arrival = pltpu.make_async_remote_copy(
                src_ref=zs.at[k], dst_ref=zr.at[k], send_sem=zssem.at[n, k], recv_sem=zrsem.at[n, k],
                device_id=far, device_id_type=MESH,
            )

            @pl.when(jnp.logical_not(jnp.logical_and(here, l == k)))
            def _():
                arrival.wait_recv()

        total = zr[0].astype(F32)
        for k in range(1, 4):
            total = total + zr[k].astype(F32)
        for copy, own in copies:

            @pl.when(jnp.logical_not(own))
            def _():
                copy.wait_send()

        return total

    order = (2, 1, 3, 0)

    def rc_pair(v):
        return rcs[y * 2 + v]

    x_pass(f_state, fb, 0, f_far)
    x_pass(f_state, fb, 1, f_far)
    pc_mid(rc_state, rcs)
    x_pass(f_state, fb, 2, f_far)
    x_pass(f_state, fb, 3, f_far)
    f_sibs += [to_sib(fb, 3), to_sib(fb, 1)]
    for copy in gx:
        copy.wait_recv()
    g_sib = same(gcol.at[:, :, c], sib)

    for copy in rc_state[1][:3]:
        copy.wait_recv()
    c_swap.wait_recv()
    cc_core = []
    for dx in order:
        partial((x + dx) % 4, cc_t, [(rcs, lambda v: cx[v])], 96, False)
        cc_core.append(rs_core(dx, cc_t, cc_ss, cc_sr))
    g_sib.wait_recv()
    for copy in rc_state[1][3:]:
        copy.wait_recv()

    def w_term(n):
        return dot(rcs[n], gcol[n // 2, pl.ds((n % 2) * 2, 2)].reshape(384, 256))

    w = w_term(0)
    for n in range(1, 8):
        w = w + w_term(n)
    ws[j] = w.astype(BF)
    w_state = pc_y(ws)
    cc_x = [rs_x(dx, cc_core[k], cc_t, cc_sr, cc_xs, cc_xr) for k, dx in enumerate(order[:3])]
    for copy in f_far:
        copy.wait_recv()
    f_sibs.append(to_sib(fb, 2))
    for k, d in enumerate((0, 3, 1, 2)):
        f_sibs[k].wait_recv()
        group(fb, yf, (x + d) % 4, 256, k == 0)
    for q, rows in enumerate(thirds):
        o_rg[rows, :] = ((yf[rows, :] + w[rows, :]) * (-keep[q])).astype(BF)
    rgs[j] = o_rg[...]
    rg_state = pc_y(rgs)
    pc_end(fs_state)
    pc_end(gs_state)
    p_swap.wait_recv()
    for t in range(4):
        partial(t, gc_t, [(fstrip, rc_pair), (gstrip, lambda v: px[v])], 64, False)

    pc_end(w_state)
    gc_core = []
    for dx in order:
        partial((x + dx) % 4, gc_t, [(ws, lambda v: cx[v])], 64, True)
        gc_core.append(rs_core(dx, gc_t, gc_ss, gc_sr))
    gc_x = [rs_x(dx, gc_core[k], gc_t, gc_sr, gc_xs, gc_xr) for k, dx in enumerate(order[:3])]
    cc_z = rs_z(0, cc_core[3], cc_x, cc_t, cc_sr, cc_xr, cc_zs, cc_zr)

    pc_end(rg_state)
    f_swap.wait_recv()
    gg_core = []
    for dx in order:
        partial((x + dx) % 4, gg_t, [(rgs, lambda v: fx[v])], 64, False)
        gg_core.append(rs_core(dx, gg_t, gg_ss, gg_sr))
    gg_x = [rs_x(dx, gg_core[k], gg_t, gg_sr, gg_xs, gg_xr) for k, dx in enumerate(order[:3])]
    gc_z = rs_z(1, gc_core[3], gc_x, gc_t, gc_sr, gc_xr, gc_zs, gc_zr)
    gg_z = rs_z(2, gg_core[3], gg_x, gg_t, gg_sr, gg_xr, gg_zs, gg_zr)
    o_gc[...] = (-rs_end(gc_z, gc_zs, gc_zr)).astype(BF)
    gcs[j] = o_gc[...]
    gc_state = pc_start(gcs)
    o_cc[...] = (px[h].astype(F32) - rs_end(cc_z, cc_zs, cc_zr)).astype(BF)
    total = pg_in[...].astype(F32) - rs_end(gg_z, gg_zs, gg_zr)
    pc_mid(gc_state, gcs)
    pc_end(gc_state)

    for n in range(8):
        panel = gcol[n // 2, pl.ds((n % 2) * 2, 2)].reshape(384, 256)
        total = total - dot(gcs[n], panel)
    o_gg[...] = total.astype(BF)
    for copy in started:
        copy.wait_send()


def rs_scratch(height, width):
    return [
        pltpu.VMEM((4, 4, 2, height, width), F32),
        pltpu.VMEM((4, 4, height, width), BF),
        pltpu.VMEM((4, 4, height, width), BF),
        pltpu.VMEM((3, 4, height, width), BF),
        pltpu.VMEM((3, 4, height, width), BF),
        pltpu.VMEM((4, height, width), BF),
        pltpu.VMEM((4, height, width), BF),
    ]


def write(*refs):
    for k in range(5):
        refs[5 + k][...] = refs[k][...]


def per_device(root, child, cpiv, gchild, groot, gpiv, blocks):
    vm = pl.BlockSpec(memory_space=pltpu.VMEM)
    shapes = [(192, 384), (96, 384), (64, 384), (192, 256), (64, 256)]
    outs = pl.pallas_call(
        kernel,
        out_shape=[jax.ShapeDtypeStruct(s, BF) for s in shapes],
        in_specs=[pl.BlockSpec(memory_space=pltpu.SMEM)] + [pl.BlockSpec(memory_space=pl.ANY)] * 6,
        out_specs=[vm] * 5,
        scratch_shapes=[
            pltpu.VMEM((192, 384), BF),
            pltpu.VMEM((192, 256), BF),
            pltpu.VMEM((2, 96, 384), BF),
            pltpu.VMEM((2, 192, 384), BF),
            pltpu.VMEM((2, 192, 256), BF),
            pltpu.VMEM((64, 256), BF),
            pltpu.VMEM((4, 4, 2, 192, 384), BF),
            pltpu.VMEM((4, 4, 2, 192, 256), BF),
            pltpu.VMEM((8, 192, 768), BF),
            pltpu.VMEM((4, 4, 2, 96, 256), BF),
            pltpu.VMEM((8, 96, 256), BF),
            pltpu.VMEM((8, 192, 256), BF),
            pltpu.VMEM((8, 192, 384), BF),
            pltpu.VMEM((8, 192, 256), BF),
            pltpu.VMEM((8, 192, 256), BF),
            pltpu.VMEM((8, 64, 384), BF),
            pltpu.VMEM((192, 384), F32),
            pltpu.VMEM((192, 256), F32),
            *rs_scratch(96, 384),
            *rs_scratch(64, 384),
            *rs_scratch(64, 256),
            pltpu.SemaphoreType.DMA((NSEM,)),
            pltpu.SemaphoreType.DMA((NSEM,)),
            pltpu.SemaphoreType.DMA((7,)),
            pltpu.SemaphoreType.DMA((3, 4)),
            pltpu.SemaphoreType.DMA((3, 4)),
        ],
        compiler_params=pltpu.CompilerParams(
            collective_id=0, has_side_effects=True, vmem_limit_bytes=62 * 2**20
        ),
        name="selected_inverse",
    )(blocks, root, child, cpiv, gchild, groot, gpiv)
    return pl.pallas_call(
        write,
        out_shape=[jax.ShapeDtypeStruct(s, BF) for s in shapes],
        in_specs=[vm] * 5,
        out_specs=[vm] * 5,
        name="write_results",
    )(*outs)


def solution(mesh):
    placed = (P("pr", "pc"),) * 6 + (P(),)
    return jax.shard_map(
        per_device,
        mesh=mesh,
        in_specs=placed,
        out_specs=(P("pr", "pc"),) * 5,
        check_vma=False,
    )
```

```python
import functools

import jax
import jax.numpy as jnp
from jax import lax
from jax.experimental import pallas as pl
from jax.experimental.pallas import tpu as pltpu
from jax.sharding import PartitionSpec as P

MESH = pl.DeviceIdType.MESH
BF = jnp.bfloat16
F32 = jnp.float32
NSEM = 160


def dot(a, b):
    return jnp.dot(a, b, preferred_element_type=F32)


def tdot(a, b):
    return lax.dot_general(a, b, (((0,), (0,)), ((), ())), preferred_element_type=F32)


def device(x, l, c, y, h):
    return (x * 8 + l * 2 + c, y * 2 + h)


def kernel(
    flags, root, child, cpiv, gchild, groot, gpiv,
    o_rc, o_cc, o_gc, o_rg, o_gg,
    craw, fraw, px, cx, fx, pg_in, cb, fb, rbuf, gcol, gstrip, fstrip, rcs, ws, rgs, gcs, yc, yf,
    cc_t, cc_ss, cc_sr, cc_xs, cc_xr, cc_zs, cc_zr,
    gc_t, gc_ss, gc_sr, gc_xs, gc_xr, gc_zs, gc_zr,
    gg_t, gg_ss, gg_sr, gg_xs, gg_xr, gg_zs, gg_zr,
    ssem, rsem, lsem, zssem, zrsem,
):
    i = lax.axis_index("pr")
    j = lax.axis_index("pc")
    x, l, c = i // 8, (i // 2) % 4, i % 2
    y, h = j // 2, j % 2
    sib = device(x, l, 1 - c, y, h)
    far = device(x, l, c, y, 1 - h)

    def at_x(d):
        return device((x + d) % 4, l, c, y, h)

    def at_y(d):
        return device(x, l, c, (y + d) % 4, h)

    def at_z(d):
        return device(x, (l + d) % 4, c, y, h)

    peers = [sib, far] + [f(d) for f in (at_x, at_y, at_z) for d in (1, 2, 3)]
    peers += [device(x, (l + d) % 4, c, y, 1 - h) for d in (1, 2, 3)]
    barrier = pltpu.get_barrier_semaphore()
    for p in peers:
        pl.semaphore_signal(barrier, inc=1, device_id=p, device_id_type=MESH)

    pulls = []
    for src, dst in (
        (child, craw), (root, rbuf.at[j]), (groot, fraw), (gchild, gcol.at[x, l, c]),
        (gchild, gstrip.at[j]), (cpiv, px.at[h]), (gpiv, pg_in),
    ):
        pull = pltpu.make_async_copy(src, dst, lsem.at[len(pulls)])
        pull.start()
        pulls.append(pull)
    keep = [jnp.where(flags[i * 3 + q] > 0, 1.0, 0.0).astype(F32) for q in range(3)]
    thirds = [slice(q * 64, q * 64 + 64) for q in range(3)]
    c_mine, f_mine = cb.at[x, l, c], fb.at[x, l, c]
    pulls[0].wait()
    for q, rows in enumerate(thirds):
        c_mine[rows, :] = (craw[rows, :].astype(F32) * keep[q]).astype(BF)
    cx[h] = c_mine[...]
    pulls[1].wait()
    pl.semaphore_wait(barrier, len(peers))

    started = []

    def send(src, dst, dev):
        n = len(started)
        copy = pltpu.make_async_remote_copy(
            src_ref=src, dst_ref=dst, send_sem=ssem.at[n], recv_sem=rsem.at[n],
            device_id=dev, device_id_type=MESH,
        )
        copy.start()
        started.append(copy)
        return copy

    def same(ref, dev):
        return send(ref, ref, dev)

    def pc_y(buf):
        return [], [same(buf.at[j], at_y(d)) for d in (1, 3, 2)]

    def pc_far(state, buf):
        state[0].append(same(buf.at[j], far))

    def pc_start(buf):
        return [same(buf.at[j], far)], [same(buf.at[j], at_y(d)) for d in (1, 3, 2)]

    def pc_mid(state, buf):
        state[0][0].wait_recv()
        state[1].extend(same(buf.at[y * 2 + 1 - h], at_y(d)) for d in (1, 3, 2))

    def pc_end(state):
        for copy in state[1]:
            copy.wait_recv()

    upper, lower = pl.ds(0, 96), pl.ds(96, 96)
    y_left, y_right = (y + 3) % 4, (y + 1) % 4

    def r_ring(hh):
        n = y * 2 + hh
        return [
            same(rbuf.at[n, upper], at_y(1)), same(rbuf.at[n, lower], at_y(3)),
            same(rbuf.at[n, upper], at_y(3)), same(rbuf.at[n, lower], at_y(1)),
        ]

    def r_pass(copies, hh):
        copies[0].wait_recv()
        copies.append(same(rbuf.at[y_left * 2 + hh, upper], at_y(1)))
        copies[1].wait_recv()
        copies.append(same(rbuf.at[y_right * 2 + hh, lower], at_y(3)))

    def r_end(copies):
        for copy in copies[2:]:
            copy.wait_recv()

    def x_start(mine):
        return [], [same(mine, at_x(1))], [same(mine, at_x(3))]

    def z_start(state, mine):
        state[0].extend(same(mine, at_z(d)) for d in (1, 3, 2))

    def z_pass(state, buf, k):
        state[0][k].wait_recv()
        got = buf.at[x, (l + 4 - (1, 3, 2)[k]) % 4, c]
        state[1].append(same(got, at_x(1)))
        state[2].append(same(got, at_x(3)))

    def x_pass(state, buf, k, into):
        lz = (l + 4 - (0, 1, 3, 2)[k]) % 4
        state[1][k].wait_recv()
        into.append(same(buf.at[(x + 3) % 4, lz, c, upper], at_x(1)))
        state[2][k].wait_recv()
        into.append(same(buf.at[(x + 1) % 4, lz, c, lower], at_x(3)))

    def to_sib(buf, d):
        return same(buf.at[(x + d) % 4, :, c], sib)

    c_state, c_far = x_start(c_mine), []
    z_start(c_state, c_mine)
    r_far_a = same(rbuf.at[j, upper], far)
    r_far_b = same(rbuf.at[j, lower], far)
    r_own = r_ring(h)
    pulls[2].wait()
    for q, rows in enumerate(thirds):
        f_mine[rows, :] = (fraw[rows, :].astype(F32) * keep[q]).astype(BF)
    fstrip[j] = f_mine[...]
    fx[h] = f_mine[...]
    for k in (3, 4, 5, 6):
        pulls[k].wait()
    z_pass(c_state, cb, 0)
    r_pass(r_own, h)
    z_pass(c_state, cb, 1)
    z_pass(c_state, cb, 2)
    c_sibs = [to_sib(cb, 0)]
    x_pass(c_state, cb, 0, c_far)
    r_far_a.wait_recv()
    n_far = y * 2 + 1 - h
    r_away = [same(rbuf.at[n_far, upper], at_y(1)), same(rbuf.at[n_far, upper], at_y(3))]
    x_pass(c_state, cb, 1, c_far)
    r_far_b.wait_recv()
    r_away += [same(rbuf.at[n_far, lower], at_y(3)), same(rbuf.at[n_far, lower], at_y(1))]
    r_away = [r_away[0], r_away[2], r_away[1], r_away[3]]
    x_pass(c_state, cb, 2, c_far)
    x_pass(c_state, cb, 3, c_far)
    c_sibs += [to_sib(cb, 3), to_sib(cb, 1)]
    gz = [same(gcol.at[x, l, c], at_z(d)) for d in (1, 3, 2)]
    r_pass(r_away, 1 - h)
    f_state, f_far = x_start(f_mine), []
    z_start(f_state, f_mine)
    fs_state, gs_state = pc_y(fstrip), pc_y(gstrip)
    for copy in gz:
        copy.wait_recv()
    gx = [same(gcol.at[x, :, c], at_x(d)) for d in (1, 3, 2)]
    for copy in c_far:
        copy.wait_recv()
    c_sibs.append(to_sib(cb, 2))
    z_pass(f_state, fb, 0)
    z_pass(f_state, fb, 1)
    r_end(r_own)
    r_end(r_away)

    def group(buf, acc, xs, width, first):
        def half(hh):
            return dot(rbuf[xs * 2 + hh], buf[xs, pl.ds(hh * 2, 2)].reshape(768, width))

        part = half(0) + half(1)
        acc[...] = part if first else acc[...] + part

    for k, d in enumerate((0, 3, 1, 2)):
        c_sibs[k].wait_recv()
        group(cb, yc, (x + d) % 4, 384, k == 0)

    for q, rows in enumerate(thirds):
        o_rc[rows, :] = (yc[rows, :] * (-keep[q])).astype(BF)
    rcs[j] = o_rc[...]
    rc_state = pc_start(rcs)

    c_swap = same(cx.at[h], far)
    p_swap = same(px.at[h], far)
    f_swap = same(fx.at[h], far)
    z_pass(f_state, fb, 2)
    f_sibs = [to_sib(fb, 0)]

    def partial(t, dst, pairs, height, add):
        strips = [(strip[t * 2 + h].T, block) for strip, block in pairs]
        for v in range(2):
            total = None
            for strip, block in strips:
                part = dot(strip, block(v))
                total = part if total is None else total + part
            total = total.reshape(2, 2, height, total.shape[-1])
            if add:
                total = dst[t, 2 * v : 2 * v + 2] - total
            dst[t, 2 * v : 2 * v + 2] = total

    def rs_core(dx, tot, ss, sr):
        t = (x + dx) % 4
        ss[t] = tot[t, :, 1 - c].astype(BF)
        return send(ss.at[t], sr.at[t], sib)

    def rs_x(dx, copy, tot, sr, xs, xr):
        t = (x + dx) % 4
        copy.wait_recv()
        xs[dx - 1] = (tot[t, :, c] + sr[t].astype(F32)).astype(BF)
        return send(xs.at[dx - 1], xr.at[dx - 1], at_x(dx))

    here = l // 2 == h

    def rs_z(n, copy, xcopies, tot, sr, xr, zs, zr):
        copy.wait_recv()
        total = tot[x, :, c] + sr[x].astype(F32)
        for xc in xcopies:
            xc.wait_recv()
        for k in range(3):
            total = total + xr[k].astype(F32)
        zs[...] = total.astype(BF)
        copies = []
        for m in (3, 2, 1, 0):
            own = jnp.logical_and(here, h * 2 + l % 2 == m)
            copy = pltpu.make_async_remote_copy(
                src_ref=zs.at[m], dst_ref=zr.at[l], send_sem=zssem.at[n, m], recv_sem=zrsem.at[n, l],
                device_id=device(x, 2 * h + m % 2, c, y, m // 2), device_id_type=MESH,
            )

            @pl.when(jnp.logical_not(own))
            def _():
                copy.start()

            @pl.when(own)
            def _():
                zr[l] = zs[m]

            copies.append((copy, own))
        return n, copies

    def rs_end(state, zs, zr):
        n, copies = state
        for k in range(4):
            arrival = pltpu.make_async_remote_copy(
                src_ref=zs.at[k], dst_ref=zr.at[k], send_sem=zssem.at[n, k], recv_sem=zrsem.at[n, k],
                device_id=far, device_id_type=MESH,
            )

            @pl.when(jnp.logical_not(jnp.logical_and(here, l == k)))
            def _():
                arrival.wait_recv()

        total = zr[0].astype(F32)
        for k in range(1, 4):
            total = total + zr[k].astype(F32)
        for copy, own in copies:

            @pl.when(jnp.logical_not(own))
            def _():
                copy.wait_send()

        return total

    order = (2, 1, 3, 0)

    def rc_pair(v):
        return rcs[y * 2 + v]

    x_pass(f_state, fb, 0, f_far)
    x_pass(f_state, fb, 1, f_far)
    pc_mid(rc_state, rcs)
    x_pass(f_state, fb, 2, f_far)
    x_pass(f_state, fb, 3, f_far)
    f_sibs += [to_sib(fb, 3), to_sib(fb, 1)]
    for copy in gx:
        copy.wait_recv()
    g_sib = same(gcol.at[:, :, c], sib)

    for copy in rc_state[1][:3]:
        copy.wait_recv()
    c_swap.wait_recv()
    cc_core = []
    for dx in order:
        partial((x + dx) % 4, cc_t, [(rcs, lambda v: cx[v])], 96, False)
        cc_core.append(rs_core(dx, cc_t, cc_ss, cc_sr))
    g_sib.wait_recv()
    for copy in rc_state[1][3:]:
        copy.wait_recv()

    def w_term(n):
        return dot(rcs[n], gcol[n // 2, pl.ds((n % 2) * 2, 2)].reshape(384, 256))

    w = w_term(0)
    for n in range(1, 8):
        w = w + w_term(n)
    ws[j] = w.astype(BF)
    w_state = pc_y(ws)
    cc_x = [rs_x(dx, cc_core[k], cc_t, cc_sr, cc_xs, cc_xr) for k, dx in enumerate(order[:3])]
    for copy in f_far:
        copy.wait_recv()
    f_sibs.append(to_sib(fb, 2))
    for k, d in enumerate((0, 3, 1, 2)):
        f_sibs[k].wait_recv()
        group(fb, yf, (x + d) % 4, 256, k == 0)
    for q, rows in enumerate(thirds):
        o_rg[rows, :] = ((yf[rows, :] + w[rows, :]) * (-keep[q])).astype(BF)
    rgs[j] = o_rg[...]
    rg_state = pc_y(rgs)
    pc_end(fs_state)
    pc_end(gs_state)
    p_swap.wait_recv()
    for t in range(4):
        partial(t, gc_t, [(fstrip, rc_pair), (gstrip, lambda v: px[v])], 64, False)

    pc_end(w_state)
    gc_core = []
    for dx in order:
        partial((x + dx) % 4, gc_t, [(ws, lambda v: cx[v])], 64, True)
        gc_core.append(rs_core(dx, gc_t, gc_ss, gc_sr))
    gc_x = [rs_x(dx, gc_core[k], gc_t, gc_sr, gc_xs, gc_xr) for k, dx in enumerate(order[:3])]
    cc_z = rs_z(0, cc_core[3], cc_x, cc_t, cc_sr, cc_xr, cc_zs, cc_zr)

    pc_end(rg_state)
    f_swap.wait_recv()
    gg_core = []
    for dx in order:
        partial((x + dx) % 4, gg_t, [(rgs, lambda v: fx[v])], 64, False)
        gg_core.append(rs_core(dx, gg_t, gg_ss, gg_sr))
    gg_x = [rs_x(dx, gg_core[k], gg_t, gg_sr, gg_xs, gg_xr) for k, dx in enumerate(order[:3])]
    gc_z = rs_z(1, gc_core[3], gc_x, gc_t, gc_sr, gc_xr, gc_zs, gc_zr)
    gg_z = rs_z(2, gg_core[3], gg_x, gg_t, gg_sr, gg_xr, gg_zs, gg_zr)
    o_gc[...] = (-rs_end(gc_z, gc_zs, gc_zr)).astype(BF)
    gcs[j] = o_gc[...]
    gc_state = pc_start(gcs)
    o_cc[...] = (px[h].astype(F32) - rs_end(cc_z, cc_zs, cc_zr)).astype(BF)
    total = pg_in[...].astype(F32) - rs_end(gg_z, gg_zs, gg_zr)
    pc_mid(gc_state, gcs)
    pc_end(gc_state)

    for n in range(8):
        panel = gcol[n // 2, pl.ds((n % 2) * 2, 2)].reshape(384, 256)
        total = total - dot(gcs[n], panel)
    o_gg[...] = total.astype(BF)
    for copy in started:
        copy.wait_send()


def rs_scratch(height, width):
    return [
        pltpu.VMEM((4, 4, 2, height, width), F32),
        pltpu.VMEM((4, 4, height, width), BF),
        pltpu.VMEM((4, 4, height, width), BF),
        pltpu.VMEM((3, 4, height, width), BF),
        pltpu.VMEM((3, 4, height, width), BF),
        pltpu.VMEM((4, height, width), BF),
        pltpu.VMEM((4, height, width), BF),
    ]


def write(*refs):
    for k in range(5):
        refs[5 + k][...] = refs[k][...]


def per_device(root, child, cpiv, gchild, groot, gpiv, blocks):
    vm = pl.BlockSpec(memory_space=pltpu.VMEM)
    shapes = [(192, 384), (96, 384), (64, 384), (192, 256), (64, 256)]
    outs = pl.pallas_call(
        kernel,
        out_shape=[jax.ShapeDtypeStruct(s, BF) for s in shapes],
        in_specs=[pl.BlockSpec(memory_space=pltpu.SMEM)] + [pl.BlockSpec(memory_space=pl.ANY)] * 6,
        out_specs=[vm] * 5,
        scratch_shapes=[
            pltpu.VMEM((192, 384), BF),
            pltpu.VMEM((192, 256), BF),
            pltpu.VMEM((2, 96, 384), BF),
            pltpu.VMEM((2, 192, 384), BF),
            pltpu.VMEM((2, 192, 256), BF),
            pltpu.VMEM((64, 256), BF),
            pltpu.VMEM((4, 4, 2, 192, 384), BF),
            pltpu.VMEM((4, 4, 2, 192, 256), BF),
            pltpu.VMEM((8, 192, 768), BF),
            pltpu.VMEM((4, 4, 2, 96, 256), BF),
            pltpu.VMEM((8, 96, 256), BF),
            pltpu.VMEM((8, 192, 256), BF),
            pltpu.VMEM((8, 192, 384), BF),
            pltpu.VMEM((8, 192, 256), BF),
            pltpu.VMEM((8, 192, 256), BF),
            pltpu.VMEM((8, 64, 384), BF),
            pltpu.VMEM((192, 384), F32),
            pltpu.VMEM((192, 256), F32),
            *rs_scratch(96, 384),
            *rs_scratch(64, 384),
            *rs_scratch(64, 256),
            pltpu.SemaphoreType.DMA((NSEM,)),
            pltpu.SemaphoreType.DMA((NSEM,)),
            pltpu.SemaphoreType.DMA((7,)),
            pltpu.SemaphoreType.DMA((3, 4)),
            pltpu.SemaphoreType.DMA((3, 4)),
        ],
        compiler_params=pltpu.CompilerParams(
            collective_id=0, has_side_effects=True, vmem_limit_bytes=62 * 2**20
        ),
        name="selected_inverse",
    )(blocks, root, child, cpiv, gchild, groot, gpiv)
    return pl.pallas_call(
        write,
        out_shape=[jax.ShapeDtypeStruct(s, BF) for s in shapes],
        in_specs=[vm] * 5,
        out_specs=[vm] * 5,
        name="write_results",
    )(*outs)


def solution(mesh):
    placed = (P("pr", "pc"),) * 6 + (P(),)
    return jax.shard_map(
        per_device,
        mesh=mesh,
        in_specs=placed,
        out_specs=(P("pr", "pc"),) * 5,
        check_vma=False,
    )
```
